32 devices in a mesh: lag: 2 (over y), row: 16 (over z, x, core).
Axes of the slice: x: 2, y: 2, z: 4, core: 2. Of those that a mesh axis runs over, the one named last changes fastest.
Arguments:
- lag_matrices: bfloat16 [8, 8192, 8192], P('lag', 'row'), may hold values from -0.0234375 to 0.0234375
- history: bfloat16 [8, 8192, 256], P('lag', 'row'), may hold values from -6 to 6
- excitation: float32 [4, 8192, 256], P(None, 'row'), may hold values from -6 to 6
- admittance: float32 [8192], P('row'), may hold values from 0.3 to 1.5
- saturation: float32 [8192], P('row'), may hold values from 0.2 to 1
Outputs:
- densities: bfloat16 [4, 8192, 256], P(None, 'row')
The draws below stay inside these ranges and needn't reach their ends.
All inputs are finite; a program needn't handle non-finite values.
Results may differ from the reference program's by a relative error of at most 0.0023.
Values may be sent and summed in bfloat16 or wider, within the bound.
No kernel may reach another device: no remote copies, remote signals or barrier semaphores. Data moves between devices by JAX's collectives and lax.ppermute only.
A program may use at most 192 MiB of HBM per device.

```python
import math
import jax
import jax.numpy as jnp
from jax import lax

UNKNOWNS = 8192
LAGS = 8
COLUMNS = 256
STEPS = 4


def steps_of(key, extent, split, low, top_value):
    def one(dim, blocks):
        draws = jax.random.uniform(jax.random.fold_in(jax.random.fold_in(key, 6), dim), (blocks,), jnp.float32, low / len(split), top_value / len(split))
        return jnp.repeat(jnp.exp(draws), extent[dim] // blocks).reshape((-1,) + (1,) * (len(extent) - dim - 1))

    factor_of = one(*split[0])
    for cut in split[1:]:
        factor_of = factor_of * one(*cut)
    return factor_of


def scatter_about(own_key, dims, width, reach, cuts=(), dtype=jnp.bfloat16):
    values = width * jax.random.normal(own_key, dims, jnp.float32)
    if cuts:
        values = values * steps_of(own_key, dims, cuts, -0.22, 0.18)
    return jnp.clip(values, -reach, reach).astype(dtype)


def setup_inputs(seed: int = 0) -> dict:
    key_list = jax.random.split(jax.random.key(seed), 6)
    return {
        "lag_matrices": scatter_about(key_list[0], (LAGS, UNKNOWNS, UNKNOWNS), (UNKNOWNS * LAGS) ** -0.5, 0.0234375, ((0, 2), (1, 16))),
        "history": scatter_about(key_list[1], (LAGS, UNKNOWNS, COLUMNS), 1.0, 6.0, ((0, 2), (1, 16))),
        "excitation": scatter_about(key_list[2], (STEPS, UNKNOWNS, COLUMNS), 1.0, 6.0, ((1, 16),), jnp.float32),
        "admittance": jnp.clip(jnp.exp(math.log(1.5) - 1.60943787 * jax.random.uniform(key_list[3], (UNKNOWNS,), jnp.float32) ** steps_of(key_list[3], (UNKNOWNS,), ((0, 16),), -0.2, 0.2)), 0.3, 1.5),
        "saturation": jnp.clip(jnp.exp(math.log(1.0) - 1.609438 * jax.random.uniform(key_list[4], (UNKNOWNS,), jnp.float32) ** steps_of(key_list[4], (UNKNOWNS,), ((0, 16),), -0.2, 0.2)), 0.2, 1.0),
    }


def reference(lag_matrices, history, excitation, admittance, saturation):
    history_now = history
    results = []
    admit_col = admittance[:, None]
    satur_col = saturation[:, None]
    for step_index in range(STEPS):

        def add_lag(lag_slot, running):
            return running + jnp.dot(lag_matrices[lag_slot], history_now[lag_slot], preferred_element_type=jnp.float32)
        scattered = lax.fori_loop(0, LAGS, add_lag, jnp.zeros((UNKNOWNS, COLUMNS), jnp.float32))
        drive = excitation[step_index] - scattered
        density = (admit_col * drive / jnp.sqrt(1.0 + (satur_col * drive) ** 2)).astype(jnp.bfloat16)
        results.append(density)
        history_now = jnp.concatenate([density[None], history_now[:-1]], axis=0)
    return jnp.stack(results)
```

```python
import functools

import jax
import jax.numpy as jnp
from jax import lax
from jax.experimental import pallas as pl
from jax.experimental.pallas import tpu as pltpu
from jax.sharding import PartitionSpec as P

VMEM_LIMIT = 40 * 1024 * 1024


def load_update(drive, admit_col, satur_col):
    return (admit_col * drive / jnp.sqrt(1.0 + (satur_col * drive) ** 2)).astype(jnp.bfloat16)


def ring_of(members):
    pairs = [(m, m + 1) for m in range(0, members, 2)]
    cycle = pairs[0::2] + pairs[1::2][::-1]
    return [m for pair in cycle for m in pair]


def place_in_ring(member, members):
    pair, core = member // 2, member % 2
    up, across = pair // 2, pair % 2
    return 2 * (up + across * (members // 2 - 1 - 2 * up)) + core


def dot(a, b):
    return jnp.dot(a, b, preferred_element_type=jnp.float32)


def params():
    return pltpu.CompilerParams(vmem_limit_bytes=VMEM_LIMIT)


def cost(z_blocks, rows, unknowns, columns, products, h_blocks):
    return pl.CostEstimate(
        flops=2 * products * rows * unknowns * columns,
        bytes_accessed=2 * z_blocks * rows * unknowns + 2 * h_blocks * unknowns * columns,
        transcendentals=0,
    )


def first_kernel(slots, z_ref, h_ref, out_ref):
    total = dot(z_ref[0], h_ref[0])
    for slot in range(1, slots):
        total += dot(z_ref[slot], h_ref[slot])

    @pl.when(pl.program_id(0) == 0)
    def _():
        out_ref[...] = total

    @pl.when(pl.program_id(0) > 0)
    def _():
        out_ref[...] += total


def first_products(members, z, h):
    slots, rows, unknowns = z.shape
    columns = h.shape[-1]
    depth, place = unknowns // members, functools.partial(place_in_ring, members=members)
    return pl.pallas_call(
        functools.partial(first_kernel, slots),
        grid=(members,),
        in_specs=[
            pl.BlockSpec((slots, rows, depth), lambda k: (0, 0, k)),
            pl.BlockSpec((slots, depth, columns), lambda k: (0, place(k), 0)),
        ],
        out_specs=pl.BlockSpec((rows, columns), lambda k: (0, 0)),
        out_shape=jax.ShapeDtypeStruct((rows, columns), jnp.float32),
        compiler_params=params(),
        cost_estimate=cost(slots, rows, unknowns, columns, slots, slots),
    )(z, h)


def later_kernel(slots, steps, *refs):
    z_refs, h_ref, outs = refs[: slots - 1], refs[slots - 1], refs[slots:]
    for shift in range(1, steps):
        total = None
        for slot in range(slots - shift):
            term = dot(z_refs[slot + shift - 1][0], h_ref[slot])
            total = term if total is None else total + term
        out_ref = outs[shift - 1]

        @pl.when(pl.program_id(0) == 0)
        def _():
            out_ref[...] = total

        @pl.when(pl.program_id(0) > 0)
        def _():
            out_ref[...] += total


def later_products(members, z, h, steps):
    slots, rows, unknowns = z.shape
    columns = h.shape[-1]
    depth, place = unknowns // members, functools.partial(place_in_ring, members=members)
    whole = pl.BlockSpec((rows, columns), lambda k: (0, 0))
    products = sum(slots - shift for shift in range(1, steps))
    return pl.pallas_call(
        functools.partial(later_kernel, slots, steps),
        grid=(members,),
        in_specs=[
            pl.BlockSpec((1, rows, depth), lambda k, slot=slot: (slot, 0, k))
            for slot in range(1, slots)
        ]
        + [pl.BlockSpec((slots - 1, depth, columns), lambda k: (0, place(k), 0))],
        out_specs=[whole] * (steps - 1),
        out_shape=[jax.ShapeDtypeStruct((rows, columns), jnp.float32)] * (steps - 1),
        compiler_params=params(),
        cost_estimate=cost(slots - 1, rows, unknowns, columns, products, slots - 1),
    )(*([z] * (slots - 1)), h)


def spread_kernel(count, *refs):
    z_refs, y_ref, accs, outs = (
        refs[:count], refs[count], refs[count + 1 : 2 * count + 1], refs[2 * count + 1 :]
    )
    for z_ref, acc_ref, out_ref in zip(z_refs, accs, outs):
        term = dot(z_ref[0], y_ref[...])

        @pl.when(pl.program_id(0) == 0)
        def _():
            out_ref[...] = acc_ref[...] + term

        @pl.when(pl.program_id(0) > 0)
        def _():
            out_ref[...] += term


def spread(members, z, y, accs, first_slot):
    _, rows, unknowns = z.shape
    columns = y.shape[-1]
    depth, place = unknowns // members, functools.partial(place_in_ring, members=members)
    count = len(accs)
    whole = pl.BlockSpec((rows, columns), lambda k: (0, 0))
    return pl.pallas_call(
        functools.partial(spread_kernel, count),
        grid=(members,),
        in_specs=[
            pl.BlockSpec((1, rows, depth), lambda k, slot=first_slot + i: (slot, 0, k))
            for i in range(count)
        ]
        + [pl.BlockSpec((depth, columns), lambda k: (place(k), 0))]
        + [whole] * count,
        out_specs=[whole] * count,
        out_shape=[jax.ShapeDtypeStruct((rows, columns), jnp.float32)] * count,
        compiler_params=params(),
        cost_estimate=cost(count, rows, unknowns, columns, count, 1),
    )(*([z] * count), y, *accs)


def step_kernel(z_ref, y_ref, acc_ref, other_ref, exc_ref, admit_ref, satur_ref, part_ref, dens_ref):
    k = pl.program_id(0)
    term = dot(z_ref[0], y_ref[...])

    @pl.when(k == 0)
    def _():
        part_ref[...] = acc_ref[...] + term

    @pl.when(k > 0)
    def _():
        part_ref[...] += term

    @pl.when(k == pl.num_programs(0) - 1)
    def _():
        drive = exc_ref[0] - (part_ref[...] + other_ref[...])
        dens_ref[...] = load_update(drive, admit_ref[...], satur_ref[...])


def step(members, z, y, acc, other, excitation, index, admit_col, satur_col):
    _, rows, unknowns = z.shape
    columns = y.shape[-1]
    depth, place = unknowns // members, functools.partial(place_in_ring, members=members)
    whole = pl.BlockSpec((rows, columns), lambda k: (0, 0))
    column = pl.BlockSpec((rows, 1), lambda k: (0, 0))
    return pl.pallas_call(
        step_kernel,
        grid=(members,),
        in_specs=[
            pl.BlockSpec((1, rows, depth), lambda k: (0, 0, k)),
            pl.BlockSpec((depth, columns), lambda k: (place(k), 0)),
            whole,
            whole,
            pl.BlockSpec((1, rows, columns), lambda k: (index, 0, 0)),
            column,
            column,
        ],
        out_specs=[whole, whole],
        out_shape=[
            jax.ShapeDtypeStruct((rows, columns), jnp.float32),
            jax.ShapeDtypeStruct((rows, columns), jnp.bfloat16),
        ],
        compiler_params=params(),
        cost_estimate=cost(1, rows, unknowns, columns, 1, 1),
    )(z, y, acc, other, excitation, admit_col, satur_col)


def gather_rows(block, axis, members):
    return lax.all_gather(block, "row", axis=axis, tiled=True, axis_index_groups=[ring_of(members)])


def two_group_body(members, lag_matrices, history, excitation, admittance, saturation):
    slots = lag_matrices.shape[0]
    steps = excitation.shape[0]
    is_first = lax.axis_index("lag") == 0
    admit_col, satur_col = admittance[:, None], saturation[:, None]
    down, up = [(1, 0)], [(0, 1)]

    incoming = lax.ppermute(history[slots - (steps - 1) :], "lag", up)
    archive = gather_rows(history, 1, members)
    first_part = first_products(members, lag_matrices, archive)
    first_other = lax.ppermute(first_part, "lag", down)

    archive, first_part, incoming = lax.optimization_barrier((archive, first_part, incoming))
    ahead = gather_rows(incoming[steps - 2], 0, members)
    parts = later_products(members, lag_matrices, archive, steps)

    density = load_update(excitation[0] - (first_part + first_other), admit_col, satur_col)
    results = [density]

    fresh = spread(members, lag_matrices, ahead, parts, 0)
    other = lax.ppermute(fresh[0], "lag", down)
    accs = [jnp.where(is_first, parts[i], fresh[min(i + 1, steps - 2)]) for i in range(steps - 1)]

    for index in range(1, steps):
        send = density
        if steps - 2 - index >= 0:
            send = jnp.where(is_first, density, incoming[steps - 2 - index])
        fresh_rows = gather_rows(send, 0, members)
        part, density = step(
            members, lag_matrices, fresh_rows, accs[0], other, excitation, index, admit_col, satur_col
        )
        results.append(density)
        if index + 1 < steps:
            other = lax.ppermute(part, "lag", down)
            fresh_rows, density = lax.optimization_barrier((fresh_rows, density))
            accs = spread(members, lag_matrices, fresh_rows, accs[1:], 1)

    early = jnp.stack(results[:-1])
    early = jnp.where(is_first, early, lax.ppermute(early, "lag", up))
    last = jnp.where(is_first, results[-1], lax.ppermute(results[-1], "lag", up))
    return jnp.concatenate([early, last[None]], axis=0)


def general_body(lag_matrices, history, excitation, admittance, saturation):
    slot_count = lag_matrices.shape[0]
    step_count = excitation.shape[0]
    lag_index = lax.axis_index("lag")
    admit_col = admittance[:, None]
    satur_col = saturation[:, None]
    archive = lax.all_gather(history, "lag", axis=0, tiled=True)
    archive = lax.all_gather(archive, "row", axis=1, tiled=True)
    results = []
    for step_index in range(step_count):
        own_slots = lax.dynamic_slice_in_dim(archive, lag_index * slot_count, slot_count, 0)
        partial_sum = jnp.einsum(
            "lrm,lmc->rc", lag_matrices, own_slots, preferred_element_type=jnp.float32
        )
        summed = lax.psum(partial_sum, "lag")
        density = load_update(excitation[step_index] - summed, admit_col, satur_col)
        results.append(density)
        if step_index + 1 < step_count:
            full_density = lax.all_gather(density, "row", axis=0, tiled=True)
            archive = jnp.concatenate([full_density[None], archive[:-1]], axis=0)
    return jnp.stack(results)


def solution(mesh):
    groups, members = mesh.shape["lag"], mesh.shape["row"]
    placed = (
        P("lag", "row", None),
        P("lag", "row", None),
        P(None, "row", None),
        P("row"),
        P("row"),
    )

    def body(lag_matrices, history, excitation, admittance, saturation):
        slots, steps = lag_matrices.shape[0], excitation.shape[0]
        chosen = general_body
        depth = lag_matrices.shape[2] // members
        if groups == 2 and members % 4 == 0 and depth % 128 == 0 and 2 < steps <= slots:
            chosen = functools.partial(two_group_body, members)
        return chosen(lag_matrices, history, excitation, admittance, saturation)

    return jax.shard_map(
        body, mesh=mesh, in_specs=placed, out_specs=P(None, "row", None), check_vma=False
    )
```

```python
import functools

import jax
import jax.numpy as jnp
from jax import lax
from jax.experimental import pallas as pl
from jax.experimental.pallas import tpu as pltpu
from jax.sharding import PartitionSpec as P

VMEM_LIMIT = 60 * 1024 * 1024


def load_update(drive, admit_col, satur_col):
    return (admit_col * drive / jnp.sqrt(1.0 + (satur_col * drive) ** 2)).astype(jnp.bfloat16)


def ring_of(pairs):
    order = list(range(pairs))
    return order[0::2] + order[1::2][::-1]


def place_in_ring(pair, pairs):
    up, across = pair // 2, pair % 2
    return up + across * (pairs - 1 - 2 * up)


def dot(a, b):
    return jnp.dot(a, b, preferred_element_type=jnp.float32)


def call(kernel, name, products, z_blocks, y_blocks, depth, **kwargs):
    rows, columns, unknowns = name
    return pl.pallas_call(
        kernel,
        compiler_params=pltpu.CompilerParams(vmem_limit_bytes=VMEM_LIMIT),
        cost_estimate=pl.CostEstimate(
            flops=2 * products * rows * unknowns * columns,
            bytes_accessed=2 * unknowns * (z_blocks * rows + y_blocks * columns),
            transcendentals=0,
        ),
        **kwargs,
    )


def add_to(out_ref, total):
    @pl.when(pl.program_id(0) == 0)
    def _():
        out_ref[...] = total

    @pl.when(pl.program_id(0) > 0)
    def _():
        out_ref[...] += total


def sizes(z, y):
    return z.shape[1], y.shape[-1], z.shape[2]


def whole(rows, columns):
    return pl.BlockSpec((rows, columns), lambda k: (0, 0))


def slots_kernel(count, *refs):
    z_refs, h_ref, out_ref = refs[:count], refs[count], refs[count + 1]
    total = dot(z_refs[0][0], h_ref[0])
    for slot in range(1, count):
        total += dot(z_refs[slot][0], h_ref[slot])
    add_to(out_ref, total)


def slots_product(pairs, z, h, shift):
    rows, columns, unknowns = shape = sizes(z, h)
    depth, count = unknowns // pairs, z.shape[0] - shift
    return call(
        functools.partial(slots_kernel, count), shape, count, count, count, depth,
        grid=(pairs,),
        in_specs=[
            pl.BlockSpec((1, rows, depth), lambda k, slot=slot: (slot, 0, k))
            for slot in range(shift, shift + count)
        ]
        + [pl.BlockSpec((count, depth, columns), lambda k: (0, place_in_ring(k, pairs), 0))],
        out_specs=whole(rows, columns),
        out_shape=jax.ShapeDtypeStruct((rows, columns), jnp.float32),
    )(*([z] * count), h)


def later_kernel(rows, count, steps, flag_ref, *refs):
    z_refs, h_ref, now_ref, more_ref = refs[:count], refs[count], refs[count + 1], refs[count + 2]
    outs, sums = refs[count + 3 : -1], refs[-1]
    k = pl.program_id(0)
    later = steps - 2

    @pl.when(k == 0)
    def _():
        sums[...] = more_ref[...]

    for slot in range(count):
        shifts = min(later, count - slot)
        stack = [z_refs[slot + shift][0] for shift in range(shifts)]
        stack = stack[0] if shifts == 1 else jnp.concatenate(stack, axis=0)
        sums[: shifts * rows] += dot(stack, h_ref[slot])

    @pl.when(k == pl.num_programs(0) - 1)
    def _():
        first = flag_ref[0] != 0
        for index, out_ref in enumerate(outs):
            ahead = min(index, later - 1)
            theirs = sums[ahead * rows : (ahead + 1) * rows]
            ours = now_ref[...] if index == 0 else sums[(index - 1) * rows : index * rows]
            out_ref[...] = jnp.where(first, ours, theirs)


def later_products(pairs, flag, z, h, steps, now, more):
    rows, columns, unknowns = shape = sizes(z, h)
    depth, count, later = unknowns // pairs, z.shape[0] - 2, steps - 2
    products = sum(min(later, count - slot) for slot in range(count))
    return call(
        functools.partial(later_kernel, rows, count, steps), shape, products, count, count, depth,
        grid=(pairs,),
        in_specs=[pl.BlockSpec(memory_space=pltpu.SMEM)]
        + [
            pl.BlockSpec((1, rows, depth), lambda k, slot=slot: (slot, 0, k))
            for slot in range(2, 2 + count)
        ]
        + [
            pl.BlockSpec((count, depth, columns), lambda k: (0, place_in_ring(k, pairs), 0)),
            whole(rows, columns),
            whole(later * rows, columns),
        ],
        out_specs=[whole(rows, columns)] * (steps - 1),
        out_shape=[jax.ShapeDtypeStruct((rows, columns), jnp.float32)] * (steps - 1),
        scratch_shapes=[pltpu.VMEM((later * rows, columns), jnp.float32)],
    )(flag, *([z] * count), h, now, more)


def ahead_kernel(rows, count, *refs):
    z_refs, y_ref, now_ref, now_out, more_out = (
        refs[:count], refs[count], refs[count + 1], refs[count + 2], refs[count + 3]
    )
    total = dot(jnp.concatenate([z_ref[0] for z_ref in z_refs], axis=0), y_ref[...])
    add_to(more_out, total[rows:])

    @pl.when(pl.program_id(0) == 0)
    def _():
        now_out[...] = now_ref[...] + total[:rows]

    @pl.when(pl.program_id(0) > 0)
    def _():
        now_out[...] += total[:rows]


def ahead_products(pairs, z, y, now, count):
    rows, columns, unknowns = shape = sizes(z, y)
    depth = unknowns // pairs
    return call(
        functools.partial(ahead_kernel, rows, count), shape, count, count, 1, depth,
        grid=(pairs,),
        in_specs=[
            pl.BlockSpec((1, rows, depth), lambda k, slot=slot: (slot, 0, k))
            for slot in range(count)
        ]
        + [
            pl.BlockSpec((depth, columns), lambda k: (place_in_ring(k, pairs), 0)),
            whole(rows, columns),
        ],
        out_specs=[whole(rows, columns), whole((count - 1) * rows, columns)],
        out_shape=[
            jax.ShapeDtypeStruct((rows, columns), jnp.float32),
            jax.ShapeDtypeStruct(((count - 1) * rows, columns), jnp.float32),
        ],
    )(*([z] * count), y, now)


def spread_kernel(rows, count, *refs):
    z_refs, y_ref = refs[:count], refs[count]
    accs, outs = refs[count + 1 : 2 * count + 1], refs[2 * count + 1 :]
    stack = [z_ref[0] for z_ref in z_refs]
    total = dot(stack[0] if count == 1 else jnp.concatenate(stack, axis=0), y_ref[...])
    for index in range(count):
        term = total[index * rows : (index + 1) * rows]

        @pl.when(pl.program_id(0) == 0)
        def _():
            outs[index][...] = accs[index][...] + term

        @pl.when(pl.program_id(0) > 0)
        def _():
            outs[index][...] += term


def spread(pairs, z, y, accs):
    rows, columns, unknowns = shape = sizes(z, y)
    depth, count = unknowns // pairs, len(accs)
    return call(
        functools.partial(spread_kernel, rows, count), shape, count, count, 1, depth,
        grid=(pairs,),
        in_specs=[
            pl.BlockSpec((1, rows, depth), lambda k, slot=slot: (slot, 0, k))
            for slot in range(1, 1 + count)
        ]
        + [pl.BlockSpec((depth, columns), lambda k: (place_in_ring(k, pairs), 0))]
        + [whole(rows, columns)] * count,
        out_specs=[whole(rows, columns)] * count,
        out_shape=[jax.ShapeDtypeStruct((rows, columns), jnp.float32)] * count,
    )(*([z] * count), y, *accs)


def step_kernel(
    pairs, flag_ref, z_ref, y_ref, base_ref, next_ref, admit_ref, satur_ref, drive_ref, send_ref,
    z_buf, y_buf, base_buf, next_buf, z_sems, y_sems, sems,
):
    depth = z_buf.shape[1] // pairs
    copies = []
    for at, pair in enumerate(ring_of(pairs)):
        across, down = pl.ds(pair * depth, depth), pl.ds(at * depth, depth)
        copies.append((
            pltpu.make_async_copy(z_ref.at[0, :, across], z_buf.at[:, across], z_sems.at[at]),
            pltpu.make_async_copy(y_ref.at[down, :], y_buf.at[down, :], y_sems.at[at]),
        ))
    for z_copy, y_copy in copies:
        z_copy.start()
        y_copy.start()
    base_copy = pltpu.make_async_copy(base_ref, base_buf, sems.at[0])
    next_copy = pltpu.make_async_copy(next_ref, next_buf, sems.at[1])
    base_copy.start()
    next_copy.start()
    for at, pair in enumerate(ring_of(pairs)):
        for copy in copies[at]:
            copy.wait()
        term = dot(z_buf[:, pair * depth : (pair + 1) * depth], y_buf[at * depth : (at + 1) * depth])
        if at == 0:
            drive_ref[...] = term
        else:
            drive_ref[...] += term
    base_copy.wait()
    next_copy.wait()
    drive = base_buf[...] - drive_ref[...]
    drive_ref[...] = drive
    density = load_update(drive, admit_ref[...], satur_ref[...])
    send_ref[...] = jnp.where(flag_ref[0] != 0, density, next_buf[...])


def step(pairs, flag, z, y, base, following, admit_col, satur_col):
    rows, columns, unknowns = shape = sizes(z, y)
    vmem, hbm = pl.BlockSpec(memory_space=pltpu.VMEM), pl.BlockSpec(memory_space=pl.ANY)
    return call(
        functools.partial(step_kernel, pairs), shape, 1, 1, 1, unknowns // pairs,
        in_specs=[pl.BlockSpec(memory_space=pltpu.SMEM), hbm, hbm, hbm, hbm, vmem, vmem],
        out_specs=[vmem, vmem],
        out_shape=[
            jax.ShapeDtypeStruct((rows, columns), jnp.float32),
            jax.ShapeDtypeStruct((rows, columns), jnp.bfloat16),
        ],
        scratch_shapes=[
            pltpu.VMEM((rows, unknowns), jnp.bfloat16),
            pltpu.VMEM((unknowns, columns), jnp.bfloat16),
            pltpu.VMEM((rows, columns), jnp.float32),
            pltpu.VMEM((rows, columns), jnp.bfloat16),
            pltpu.SemaphoreType.DMA((pairs,)),
            pltpu.SemaphoreType.DMA((pairs,)),
            pltpu.SemaphoreType.DMA((2,)),
        ],
    )(flag, z, y, base, following, admit_col, satur_col)


def gather_rows(pairs, block, axis):
    order = [2 * pair + core for pair in ring_of(pairs) for core in (0, 1)]
    return lax.all_gather(block, "row", axis=axis, tiled=True, axis_index_groups=[order])


def two_group_body(pairs, lag_matrices, history, excitation, admittance, saturation):
    z, steps = lag_matrices, excitation.shape[0]
    slots = z.shape[0]
    is_first = lax.axis_index("lag") == 0
    flag = is_first.astype(jnp.int32)[None]
    admit_col, satur_col = admittance[:, None], saturation[:, None]
    down, up = [(1, 0)], [(0, 1)]

    incoming = lax.ppermute(history[slots - (steps - 1) :], "lag", up)
    archive = gather_rows(pairs, history, 1)
    archive, incoming = lax.optimization_barrier((archive, incoming))
    ahead = gather_rows(pairs, incoming[steps - 2], 0)

    first_part = slots_product(pairs, z, archive, 0)
    first_other = lax.ppermute(first_part, "lag", down)
    archive, first_part = lax.optimization_barrier((archive, first_part))
    now = slots_product(pairs, z, archive, 1)
    now, first_part = lax.optimization_barrier((now, first_part))
    density = load_update(excitation[0] - (first_part + first_other), admit_col, satur_col)
    send = jnp.where(is_first, density, incoming[steps - 3])
    results = [send]
    fresh = gather_rows(pairs, send, 0)

    ahead, send = lax.optimization_barrier((ahead, send))
    now, more = ahead_products(pairs, z, ahead, now, steps - 1)
    other = lax.ppermute(-now, "lag", down)
    archive, now, more = lax.optimization_barrier((archive, now, more))
    accs = later_products(pairs, flag, z, archive, steps, now, more)

    for index in range(1, steps):
        base = jnp.where(is_first, excitation[index] + other, 0.0) - accs[0]
        following = incoming[max(steps - 3 - index, 0)]
        drive, send = step(pairs, flag, z, fresh, base, following, admit_col, satur_col)
        results.append(send)
        if index + 1 < steps:
            rows_before = fresh
            fresh = gather_rows(pairs, send, 0)
            other = lax.ppermute(drive, "lag", down)
            rows_before, send = lax.optimization_barrier((rows_before, send))
            accs = spread(pairs, z, rows_before, accs[1:])

    early = jnp.stack(results[:-1])
    early = jnp.where(is_first, early, lax.ppermute(early, "lag", up))
    last = jnp.where(is_first, results[-1], lax.ppermute(results[-1], "lag", up))
    return jnp.concatenate([early, last[None]], axis=0)


def general_body(lag_matrices, history, excitation, admittance, saturation):
    slot_count = lag_matrices.shape[0]
    step_count = excitation.shape[0]
    lag_index = lax.axis_index("lag")
    admit_col = admittance[:, None]
    satur_col = saturation[:, None]
    archive = lax.all_gather(history, "lag", axis=0, tiled=True)
    archive = lax.all_gather(archive, "row", axis=1, tiled=True)
    results = []
    for step_index in range(step_count):
        own_slots = lax.dynamic_slice_in_dim(archive, lag_index * slot_count, slot_count, 0)
        partial_sum = jnp.einsum(
            "lrm,lmc->rc", lag_matrices, own_slots, preferred_element_type=jnp.float32
        )
        summed = lax.psum(partial_sum, "lag")
        density = load_update(excitation[step_index] - summed, admit_col, satur_col)
        results.append(density)
        if step_index + 1 < step_count:
            full_density = lax.all_gather(density, "row", axis=0, tiled=True)
            archive = jnp.concatenate([full_density[None], archive[:-1]], axis=0)
    return jnp.stack(results)


def solution(mesh):
    groups, members = mesh.shape["lag"], mesh.shape["row"]
    placed = (
        P("lag", "row", None),
        P("lag", "row", None),
        P(None, "row", None),
        P("row"),
        P("row"),
    )

    def body(lag_matrices, history, excitation, admittance, saturation):
        slots, steps = lag_matrices.shape[0], excitation.shape[0]
        chosen = general_body
        depth = lag_matrices.shape[2] // members
        if groups == 2 and members % 4 == 0 and depth % 128 == 0 and 2 < steps <= slots:
            chosen = functools.partial(two_group_body, members // 2)
        return chosen(lag_matrices, history, excitation, admittance, saturation)

    return jax.shard_map(
        body, mesh=mesh, in_specs=placed, out_specs=P(None, "row", None), check_vma=False
    )
```

```python
import functools
import math

import jax
import jax.numpy as jnp
from jax import lax
from jax.experimental import pallas as pl
from jax.experimental.pallas import tpu as pltpu
from jax.sharding import PartitionSpec as P

VMEM_LIMIT = 60 * 1024 * 1024


def load_update(drive, admit_col, satur_col):
    return (admit_col * drive * lax.rsqrt(1.0 + (satur_col * drive) ** 2)).astype(jnp.bfloat16)


def ring_of(pairs):
    order = list(range(pairs))
    return order[0::2] + order[1::2][::-1]


def place_in_ring(pair, pairs):
    up, across = pair // 2, pair % 2
    return up + across * (pairs - 1 - 2 * up)


def dot(a, b):
    return jnp.dot(a, b, preferred_element_type=jnp.float32)


def call(kernel, shape, products, z_blocks, y_blocks, **kwargs):
    rows, columns, unknowns = shape
    return pl.pallas_call(
        kernel,
        compiler_params=pltpu.CompilerParams(vmem_limit_bytes=VMEM_LIMIT),
        cost_estimate=pl.CostEstimate(
            flops=2 * products * rows * unknowns * columns,
            bytes_accessed=2 * unknowns * (z_blocks * rows + y_blocks * columns),
            transcendentals=0,
        ),
        **kwargs,
    )


def add_to(out_ref, total):
    @pl.when(pl.program_id(0) == 0)
    def _():
        out_ref[...] = total

    @pl.when(pl.program_id(0) > 0)
    def _():
        out_ref[...] += total


def sizes(z, y):
    return z.shape[1], y.shape[-1], z.shape[2]


def whole(rows, columns):
    return pl.BlockSpec((rows, columns), lambda k: (0, 0))


def z_spec(rows, depth, slot):
    return pl.BlockSpec((1, rows, depth), lambda k: (slot, 0, k))


def h_spec(depth, columns, first, count, pairs):
    return pl.BlockSpec((count, depth, columns), lambda k: (first, place_in_ring(k, pairs), 0))


def y_spec(depth, columns, pairs):
    return pl.BlockSpec((depth, columns), lambda k: (place_in_ring(k, pairs), 0))


def stacked(z_refs):
    if len(z_refs) == 1:
        return z_refs[0][0]
    return jnp.concatenate([z_ref[0] for z_ref in z_refs], axis=0)


def slots_kernel(count, *refs):
    z_refs, h_ref, out_ref = refs[:count], refs[count], refs[count + 1]
    total = dot(z_refs[0][0], h_ref[0])
    for slot in range(1, count):
        total += dot(z_refs[slot][0], h_ref[slot])
    add_to(out_ref, total)


def slots_product(pairs, z, h, shift, count):
    rows, columns, unknowns = shape = sizes(z, h)
    depth = unknowns // pairs
    return call(
        functools.partial(slots_kernel, count), shape, count, count, count,
        grid=(pairs,),
        in_specs=[z_spec(rows, depth, slot) for slot in range(shift, shift + count)]
        + [h_spec(depth, columns, 0, count, pairs)],
        out_specs=whole(rows, columns),
        out_shape=jax.ShapeDtypeStruct((rows, columns), jnp.float32),
    )(*([z] * count), h)


def next_kernel(z_new_ref, y_ref, z_old_ref, h_ref, part_ref, out_ref):
    total = dot(z_new_ref[0], y_ref[...]) + dot(z_old_ref[0], h_ref[0])

    @pl.when(pl.program_id(0) == 0)
    def _():
        out_ref[...] = -part_ref[...] - total

    @pl.when(pl.program_id(0) > 0)
    def _():
        out_ref[...] -= total


def next_product(pairs, z, y, h, slot, part):
    rows, columns, unknowns = shape = sizes(z, y)
    depth = unknowns // pairs
    return call(
        next_kernel, shape, 2, 2, 2,
        grid=(pairs,),
        in_specs=[
            z_spec(rows, depth, 0),
            y_spec(depth, columns, pairs),
            z_spec(rows, depth, slot + 1),
            h_spec(depth, columns, slot, 1, pairs),
            whole(rows, columns),
        ],
        out_specs=whole(rows, columns),
        out_shape=jax.ShapeDtypeStruct((rows, columns), jnp.float32),
    )(z, y, z, h, part)


def later_kernel(rows, low, high, top, *refs):
    z_refs, y_ref, h_ref, outs, sums = refs[:top], refs[top], refs[top + 1], refs[top + 2 : -1], refs[-1]
    k = pl.program_id(0)

    @pl.when(k == 0)
    def _():
        sums[...] = jnp.zeros_like(sums)

    sums[...] -= dot(stacked(z_refs[: high - low]), y_ref[...])
    for slot in range(h_ref.shape[0]):
        stack = z_refs[slot + 1 : min(slot + 1 + high - low, top)]
        sums[: len(stack) * rows] -= dot(stacked(stack), h_ref[slot])

    @pl.when(k == pl.num_programs(0) - 1)
    def _():
        for index, out_ref in enumerate(outs):
            out_ref[...] = sums[index * rows : (index + 1) * rows]


def later_products(pairs, z, y, h, low, high):
    rows, columns, unknowns = shape = sizes(z, h)
    depth, top = unknowns // pairs, z.shape[0] - 1 - low
    count = max(top - 1, 1)
    products = high - low + sum(min(high - low, top - 1 - slot) for slot in range(top - 1))
    return call(
        functools.partial(later_kernel, rows, low, high, top), shape, products, top, count + 1,
        grid=(pairs,),
        in_specs=[z_spec(rows, depth, slot) for slot in range(low + 1, low + 1 + top)]
        + [y_spec(depth, columns, pairs), h_spec(depth, columns, 0, count, pairs)],
        out_specs=[whole(rows, columns)] * (high - low),
        out_shape=[jax.ShapeDtypeStruct((rows, columns), jnp.float32)] * (high - low),
        scratch_shapes=[pltpu.VMEM(((high - low) * rows, columns), jnp.float32)],
    )(*([z] * top), y, h)


def spread_kernel(rows, count, *refs):
    z_refs, y_ref = refs[:count], refs[count]
    accs, outs = refs[count + 1 : 2 * count + 1], refs[2 * count + 1 :]
    total = dot(stacked(z_refs), y_ref[...])
    for index in range(count):
        term = total[index * rows : (index + 1) * rows]

        @pl.when(pl.program_id(0) == 0)
        def _():
            outs[index][...] = accs[index][...] - term

        @pl.when(pl.program_id(0) > 0)
        def _():
            outs[index][...] -= term


def spread(pairs, z, y, accs):
    rows, columns, unknowns = shape = sizes(z, y)
    depth, count = unknowns // pairs, len(accs)
    return call(
        functools.partial(spread_kernel, rows, count), shape, count, count, 1,
        grid=(pairs,),
        in_specs=[z_spec(rows, depth, slot) for slot in range(1, 1 + count)]
        + [y_spec(depth, columns, pairs)]
        + [whole(rows, columns)] * count,
        out_specs=[whole(rows, columns)] * count,
        out_shape=[jax.ShapeDtypeStruct((rows, columns), jnp.float32)] * count,
    )(*([z] * count), y, *accs)


def step_kernel(
    pairs, flag_ref, z_ref, y_ref, base_ref, next_ref, loads_ref, drive_ref, send_ref,
    z_buf, y_buf, base_buf, next_buf, loads_buf, drive_buf, send_buf, z_sems, y_sems, sems,
):
    depth = z_buf.shape[1] // pairs
    copies = []
    for at, pair in enumerate(ring_of(pairs)):
        across, down = pl.ds(pair * depth, depth), pl.ds(at * depth, depth)
        copies.append((
            pltpu.make_async_copy(z_ref.at[0, :, across], z_buf.at[:, across], z_sems.at[at]),
            pltpu.make_async_copy(y_ref.at[down, :], y_buf.at[down, :], y_sems.at[at]),
        ))
    for z_copy, y_copy in copies:
        z_copy.start()
        y_copy.start()
    small = [
        pltpu.make_async_copy(base_ref, base_buf, sems.at[0]),
        pltpu.make_async_copy(next_ref, next_buf, sems.at[1]),
        pltpu.make_async_copy(loads_ref, loads_buf, sems.at[2]),
    ]
    for copy in small:
        copy.start()
    for at, pair in enumerate(ring_of(pairs)):
        for copy in copies[at]:
            copy.wait()
        term = dot(z_buf[:, pair * depth : (pair + 1) * depth], y_buf[at * depth : (at + 1) * depth])
        if at == 0:
            drive_buf[...] = term
        else:
            drive_buf[...] += term
    for copy in small:
        copy.wait()
    drive_buf[...] = base_buf[...] - drive_buf[...]
    drive_copy = pltpu.make_async_copy(drive_buf, drive_ref, sems.at[3])
    drive_copy.start()
    first = flag_ref[0] != 0
    lanes = loads_buf.shape[2]
    for start in range(0, drive_buf.shape[1], lanes):
        part = pl.ds(start, lanes)
        density = load_update(drive_buf[:, part], loads_buf[0], loads_buf[1])
        send_buf[:, part] = jnp.where(first, density, next_buf[:, part])
    send_copy = pltpu.make_async_copy(send_buf, send_ref, sems.at[4])
    send_copy.start()
    send_copy.wait()
    drive_copy.wait()


def step(pairs, flag, z, y, base, following, loads):
    rows, columns, unknowns = shape = sizes(z, y)
    hbm = pl.BlockSpec(memory_space=pl.ANY)
    return call(
        functools.partial(step_kernel, pairs), shape, 1, 1, 1,
        in_specs=[pl.BlockSpec(memory_space=pltpu.SMEM)] + [hbm] * 5,
        out_specs=[hbm, hbm],
        out_shape=[
            jax.ShapeDtypeStruct((rows, columns), jnp.float32),
            jax.ShapeDtypeStruct((rows, columns), jnp.bfloat16),
        ],
        scratch_shapes=[
            pltpu.VMEM((rows, unknowns), jnp.bfloat16),
            pltpu.VMEM((unknowns, columns), jnp.bfloat16),
            pltpu.VMEM((rows, columns), jnp.float32),
            pltpu.VMEM((rows, columns), jnp.bfloat16),
            pltpu.VMEM(loads.shape, jnp.float32),
            pltpu.VMEM((rows, columns), jnp.float32),
            pltpu.VMEM((rows, columns), jnp.bfloat16),
            pltpu.SemaphoreType.DMA((pairs,)),
            pltpu.SemaphoreType.DMA((pairs,)),
            pltpu.SemaphoreType.DMA((5,)),
        ],
    )(flag, z, y, base, following, loads)


def gather_rows(pairs, block, axis):
    order = [2 * pair + core for pair in ring_of(pairs) for core in (0, 1)]
    return lax.all_gather(block, "row", axis=axis, tiled=True, axis_index_groups=[order])


def two_group_body(pairs, lag_matrices, history, excitation, admittance, saturation):
    z, steps = lag_matrices, excitation.shape[0]
    slots = z.shape[0]
    is_first = lax.axis_index("lag") == 0
    flag = is_first.astype(jnp.int32)[None]
    admit_col, satur_col = admittance[:, None], saturation[:, None]
    lanes = math.gcd(128, excitation.shape[-1])
    loads = jnp.broadcast_to(jnp.stack([admit_col, satur_col]), (2, admit_col.shape[0], lanes))
    down, up = [(1, 0)], [(0, 1)]

    incoming = lax.ppermute(history[slots - (steps - 1) :], "lag", up)
    archive = gather_rows(pairs, history, 1)
    archive, incoming = lax.optimization_barrier((archive, incoming))
    ahead = gather_rows(pairs, incoming[steps - 2], 0)

    first_part = slots_product(pairs, z, archive, 0, slots)
    first_other = lax.ppermute(first_part, "lag", down)
    archive, first_part = lax.optimization_barrier((archive, first_part))
    part = slots_product(pairs, z, archive, 1, slots - 2)
    loads, part, first_part = lax.optimization_barrier((loads, part, first_part))
    density = load_update(excitation[0] - (first_part + first_other), admit_col, satur_col)
    send = jnp.where(is_first, density, incoming[steps - 3])
    results = [send]
    fresh = gather_rows(pairs, send, 0)

    ahead, send = lax.optimization_barrier((ahead, send))
    own = next_product(pairs, z, ahead, archive, slots - 2, part)
    other = lax.ppermute(own, "lag", down)
    archive, own = lax.optimization_barrier((archive, own))
    (theirs,) = later_products(pairs, z, ahead, archive, 0, 1)
    accs = []

    for index in range(1, steps):
        base = jnp.where(is_first, excitation[index] + other + own, theirs)
        coming = incoming[max(steps - 3 - index, 0)]
        drive, send = step(pairs, flag, z, fresh, base, coming, loads)
        results.append(send)
        if index + 1 < steps:
            rows_before = fresh
            fresh = gather_rows(pairs, send, 0)
            other = lax.ppermute(drive, "lag", down)
            rows_before, ahead, archive, send = lax.optimization_barrier(
                (rows_before, ahead, archive, send)
            )
            if index == 1:
                sums = [theirs] + list(later_products(pairs, z, ahead, archive, 1, steps - 2))
                accs = [
                    jnp.where(is_first, mine, sums[min(i + 1, steps - 3)])
                    for i, mine in enumerate(sums)
                ]
            accs = spread(pairs, z, rows_before, accs)
            own = theirs = accs[0]
            accs = accs[1:]

    early = jnp.stack(results[:-1])
    early = jnp.where(is_first, early, lax.ppermute(early, "lag", up))
    last = jnp.where(is_first, results[-1], lax.ppermute(results[-1], "lag", up))
    whole_run = jnp.concatenate([early, early[:1]], axis=0)
    return lax.dynamic_update_slice(whole_run, last[None], (steps - 1, 0, 0))


def general_body(lag_matrices, history, excitation, admittance, saturation):
    slot_count = lag_matrices.shape[0]
    step_count = excitation.shape[0]
    lag_index = lax.axis_index("lag")
    admit_col = admittance[:, None]
    satur_col = saturation[:, None]
    archive = lax.all_gather(history, "lag", axis=0, tiled=True)
    archive = lax.all_gather(archive, "row", axis=1, tiled=True)
    results = []
    for step_index in range(step_count):
        own_slots = lax.dynamic_slice_in_dim(archive, lag_index * slot_count, slot_count, 0)
        partial_sum = jnp.einsum(
            "lrm,lmc->rc", lag_matrices, own_slots, preferred_element_type=jnp.float32
        )
        summed = lax.psum(partial_sum, "lag")
        density = load_update(excitation[step_index] - summed, admit_col, satur_col)
        results.append(density)
        if step_index + 1 < step_count:
            full_density = lax.all_gather(density, "row", axis=0, tiled=True)
            archive = jnp.concatenate([full_density[None], archive[:-1]], axis=0)
    return jnp.stack(results)


def solution(mesh):
    groups, members = mesh.shape["lag"], mesh.shape["row"]
    placed = (
        P("lag", "row", None),
        P("lag", "row", None),
        P(None, "row", None),
        P("row"),
        P("row"),
    )

    def body(lag_matrices, history, excitation, admittance, saturation):
        slots, steps = lag_matrices.shape[0], excitation.shape[0]
        chosen = general_body
        depth = lag_matrices.shape[2] // members
        if groups == 2 and members % 4 == 0 and depth % 128 == 0 and 2 < steps <= slots:
            chosen = functools.partial(two_group_body, members // 2)
        return chosen(lag_matrices, history, excitation, admittance, saturation)

    return jax.shard_map(
        body, mesh=mesh, in_specs=placed, out_specs=P(None, "row", None), check_vma=False
    )
```

```python
import functools
import math

import jax
import jax.numpy as jnp
from jax import lax
from jax.experimental import pallas as pl
from jax.experimental.pallas import tpu as pltpu
from jax.sharding import PartitionSpec as P

VMEM_LIMIT = 60 * 1024 * 1024


def load_update(drive, admit_col, satur_col):
    return (admit_col * drive * lax.rsqrt(1.0 + (satur_col * drive) ** 2)).astype(jnp.bfloat16)


def ring_of(pairs):
    order = list(range(pairs))
    return order[0::2] + order[1::2][::-1]


def place_in_ring(pair, pairs):
    up, across = pair // 2, pair % 2
    return up + across * (pairs - 1 - 2 * up)


def dot(a, b):
    return jnp.dot(a, b, preferred_element_type=jnp.float32)


def call(kernel, shape, products, z_blocks, y_blocks, **kwargs):
    rows, columns, unknowns = shape
    return pl.pallas_call(
        kernel,
        compiler_params=pltpu.CompilerParams(vmem_limit_bytes=VMEM_LIMIT),
        cost_estimate=pl.CostEstimate(
            flops=2 * products * rows * unknowns * columns,
            bytes_accessed=2 * unknowns * (z_blocks * rows + y_blocks * columns),
            transcendentals=0,
        ),
        **kwargs,
    )


def add_to(out_ref, total):
    @pl.when(pl.program_id(0) == 0)
    def _():
        out_ref[...] = total

    @pl.when(pl.program_id(0) > 0)
    def _():
        out_ref[...] += total


def sizes(z, y):
    return z.shape[1], y.shape[-1], z.shape[2]


def whole(rows, columns):
    return pl.BlockSpec((rows, columns), lambda k: (0, 0))


def z_spec(rows, depth, slot):
    return pl.BlockSpec((1, rows, depth), lambda k: (slot, 0, k))


def h_spec(depth, columns, first, count, pairs):
    return pl.BlockSpec((count, depth, columns), lambda k: (first, place_in_ring(k, pairs), 0))


def y_spec(depth, columns, pairs):
    return pl.BlockSpec((depth, columns), lambda k: (place_in_ring(k, pairs), 0))


def stacked(z_refs):
    if len(z_refs) == 1:
        return z_refs[0][0]
    return jnp.concatenate([z_ref[0] for z_ref in z_refs], axis=0)


def slots_kernel(count, *refs):
    z_refs, h_ref, out_ref = refs[:count], refs[count], refs[count + 1]
    total = dot(z_refs[0][0], h_ref[0])
    for slot in range(1, count):
        total += dot(z_refs[slot][0], h_ref[slot])
    add_to(out_ref, total)


def slots_product(pairs, z, h, shift, count):
    rows, columns, unknowns = shape = sizes(z, h)
    depth = unknowns // pairs
    return call(
        functools.partial(slots_kernel, count), shape, count, count, count,
        grid=(pairs,),
        in_specs=[z_spec(rows, depth, slot) for slot in range(shift, shift + count)]
        + [h_spec(depth, columns, 0, count, pairs)],
        out_specs=whole(rows, columns),
        out_shape=jax.ShapeDtypeStruct((rows, columns), jnp.float32),
    )(*([z] * count), h)


def next_kernel(z_new_ref, y_ref, z_old_ref, h_ref, part_ref, out_ref):
    total = dot(z_new_ref[0], y_ref[...]) + dot(z_old_ref[0], h_ref[0])

    @pl.when(pl.program_id(0) == 0)
    def _():
        out_ref[...] = -part_ref[...] - total

    @pl.when(pl.program_id(0) > 0)
    def _():
        out_ref[...] -= total


def next_product(pairs, z, y, h, slot, part):
    rows, columns, unknowns = shape = sizes(z, y)
    depth = unknowns // pairs
    return call(
        next_kernel, shape, 2, 2, 2,
        grid=(pairs,),
        in_specs=[
            z_spec(rows, depth, 0),
            y_spec(depth, columns, pairs),
            z_spec(rows, depth, slot + 1),
            h_spec(depth, columns, slot, 1, pairs),
            whole(rows, columns),
        ],
        out_specs=whole(rows, columns),
        out_shape=jax.ShapeDtypeStruct((rows, columns), jnp.float32),
    )(z, y, z, h, part)


def later_kernel(rows, low, high, top, *refs):
    z_refs, y_ref, h_ref, outs, sums = refs[:top], refs[top], refs[top + 1], refs[top + 2 : -1], refs[-1]
    k = pl.program_id(0)

    @pl.when(k == 0)
    def _():
        sums[...] = jnp.zeros_like(sums)

    sums[...] -= dot(stacked(z_refs[: high - low]), y_ref[...])
    for slot in range(h_ref.shape[0]):
        stack = z_refs[slot + 1 : min(slot + 1 + high - low, top)]
        sums[: len(stack) * rows] -= dot(stacked(stack), h_ref[slot])

    @pl.when(k == pl.num_programs(0) - 1)
    def _():
        for index, out_ref in enumerate(outs):
            out_ref[...] = sums[index * rows : (index + 1) * rows]


def later_products(pairs, z, y, h, low, high):
    rows, columns, unknowns = shape = sizes(z, h)
    depth, top = unknowns // pairs, z.shape[0] - 1 - low
    count = max(top - 1, 1)
    products = high - low + sum(min(high - low, top - 1 - slot) for slot in range(top - 1))
    return call(
        functools.partial(later_kernel, rows, low, high, top), shape, products, top, count + 1,
        grid=(pairs,),
        in_specs=[z_spec(rows, depth, slot) for slot in range(low + 1, low + 1 + top)]
        + [y_spec(depth, columns, pairs), h_spec(depth, columns, 0, count, pairs)],
        out_specs=[whole(rows, columns)] * (high - low),
        out_shape=[jax.ShapeDtypeStruct((rows, columns), jnp.float32)] * (high - low),
        scratch_shapes=[pltpu.VMEM(((high - low) * rows, columns), jnp.float32)],
    )(*([z] * top), y, h)


def spread_kernel(rows, count, *refs):
    z_refs, y_ref = refs[:count], refs[count]
    accs, outs = refs[count + 1 : 2 * count + 1], refs[2 * count + 1 :]
    total = dot(stacked(z_refs), y_ref[...])
    for index in range(count):
        term = total[index * rows : (index + 1) * rows]

        @pl.when(pl.program_id(0) == 0)
        def _():
            outs[index][...] = accs[index][...] - term

        @pl.when(pl.program_id(0) > 0)
        def _():
            outs[index][...] -= term


def spread(pairs, z, y, accs):
    rows, columns, unknowns = shape = sizes(z, y)
    depth, count = unknowns // pairs, len(accs)
    return call(
        functools.partial(spread_kernel, rows, count), shape, count, count, 1,
        grid=(pairs,),
        in_specs=[z_spec(rows, depth, slot) for slot in range(1, 1 + count)]
        + [y_spec(depth, columns, pairs)]
        + [whole(rows, columns)] * count,
        out_specs=[whole(rows, columns)] * count,
        out_shape=[jax.ShapeDtypeStruct((rows, columns), jnp.float32)] * count,
    )(*([z] * count), y, *accs)


def step_kernel(
    pairs, flag_ref, z_ref, y_ref, base_ref, next_ref, loads_ref, drive_ref, send_ref,
    z_buf, y_buf, base_buf, next_buf, loads_buf, drive_buf, send_buf, z_sems, y_sems, sems,
):
    depth = z_buf.shape[1] // pairs
    copies = []
    for at, pair in enumerate(ring_of(pairs)):
        across, down = pl.ds(pair * depth, depth), pl.ds(at * depth, depth)
        copies.append((
            pltpu.make_async_copy(z_ref.at[0, :, across], z_buf.at[:, across], z_sems.at[at]),
            pltpu.make_async_copy(y_ref.at[down, :], y_buf.at[down, :], y_sems.at[at]),
        ))
    for z_copy, y_copy in copies:
        z_copy.start()
        y_copy.start()
    small = [
        pltpu.make_async_copy(base_ref, base_buf, sems.at[0]),
        pltpu.make_async_copy(next_ref, next_buf, sems.at[1]),
        pltpu.make_async_copy(loads_ref, loads_buf, sems.at[2]),
    ]
    for copy in small:
        copy.start()
    for at, pair in enumerate(ring_of(pairs)):
        for copy in copies[at]:
            copy.wait()
        term = dot(z_buf[:, pair * depth : (pair + 1) * depth], y_buf[at * depth : (at + 1) * depth])
        if at == 0:
            drive_buf[...] = term
        else:
            drive_buf[...] += term
    for copy in small:
        copy.wait()
    drive_buf[...] = base_buf[...] - drive_buf[...]
    drive_copy = pltpu.make_async_copy(drive_buf, drive_ref, sems.at[3])
    drive_copy.start()
    first = flag_ref[0] != 0
    lanes = loads_buf.shape[2]
    for start in range(0, drive_buf.shape[1], lanes):
        part = pl.ds(start, lanes)
        density = load_update(drive_buf[:, part], loads_buf[0], loads_buf[1])
        send_buf[:, part] = jnp.where(first, density, next_buf[:, part])
    send_copy = pltpu.make_async_copy(send_buf, send_ref, sems.at[4])
    send_copy.start()
    send_copy.wait()
    drive_copy.wait()


def step(pairs, flag, z, y, base, following, loads):
    rows, columns, unknowns = shape = sizes(z, y)
    hbm = pl.BlockSpec(memory_space=pl.ANY)
    return call(
        functools.partial(step_kernel, pairs), shape, 1, 1, 1,
        in_specs=[pl.BlockSpec(memory_space=pltpu.SMEM)] + [hbm] * 5,
        out_specs=[hbm, hbm],
        out_shape=[
            jax.ShapeDtypeStruct((rows, columns), jnp.float32),
            jax.ShapeDtypeStruct((rows, columns), jnp.bfloat16),
        ],
        scratch_shapes=[
            pltpu.VMEM((rows, unknowns), jnp.bfloat16),
            pltpu.VMEM((unknowns, columns), jnp.bfloat16),
            pltpu.VMEM((rows, columns), jnp.float32),
            pltpu.VMEM((rows, columns), jnp.bfloat16),
            pltpu.VMEM(loads.shape, jnp.float32),
            pltpu.VMEM((rows, columns), jnp.float32),
            pltpu.VMEM((rows, columns), jnp.bfloat16),
            pltpu.SemaphoreType.DMA((pairs,)),
            pltpu.SemaphoreType.DMA((pairs,)),
            pltpu.SemaphoreType.DMA((5,)),
        ],
    )(flag, z, y, base, following, loads)


def gather_rows(pairs, block, axis):
    order = [2 * pair + core for pair in ring_of(pairs) for core in (0, 1)]
    return lax.all_gather(block, "row", axis=axis, tiled=True, axis_index_groups=[order])


def two_group_body(pairs, lag_matrices, history, excitation, admittance, saturation):
    z, steps = lag_matrices, excitation.shape[0]
    slots = z.shape[0]
    is_first = lax.axis_index("lag") == 0
    flag = is_first.astype(jnp.int32)[None]
    admit_col, satur_col = admittance[:, None], saturation[:, None]
    lanes = math.gcd(128, excitation.shape[-1])
    loads = jnp.broadcast_to(jnp.stack([admit_col, satur_col]), (2, admit_col.shape[0], lanes))
    down, up = [(1, 0)], [(0, 1)]

    incoming = lax.ppermute(history[slots - (steps - 1) :], "lag", up)
    archive = gather_rows(pairs, history, 1)
    archive, *incoming = lax.optimization_barrier((archive, *incoming))
    ahead = gather_rows(pairs, incoming[steps - 2], 0)

    first_part = slots_product(pairs, z, archive, 0, slots)
    first_other = lax.ppermute(first_part, "lag", down)
    archive, first_part = lax.optimization_barrier((archive, first_part))
    part = slots_product(pairs, z, archive, 1, slots - 2)
    part, first_part = lax.optimization_barrier((part, first_part))
    density = load_update(excitation[0] - (first_part + first_other), admit_col, satur_col)
    send = jnp.where(is_first, density, incoming[steps - 3])
    results = [send]
    fresh = gather_rows(pairs, send, 0)

    ahead, send = lax.optimization_barrier((ahead, send))
    own = next_product(pairs, z, ahead, archive, slots - 2, part)
    other = lax.ppermute(own, "lag", down)
    archive, own = lax.optimization_barrier((archive, own))
    (theirs,) = later_products(pairs, z, ahead, archive, 0, 1)
    theirs, loads = lax.optimization_barrier((theirs, loads))
    accs = []

    for index in range(1, steps):
        base = jnp.where(is_first, excitation[index] + other + own, theirs)
        coming = incoming[max(steps - 3 - index, 0)]
        drive, send = step(pairs, flag, z, fresh, base, coming, loads)
        results.append(send)
        if index + 1 < steps:
            rows_before = fresh
            fresh = gather_rows(pairs, send, 0)
            other = lax.ppermute(drive, "lag", down)
            rows_before, ahead, archive, send = lax.optimization_barrier(
                (rows_before, ahead, archive, send)
            )
            if index == 1:
                sums = [theirs] + list(later_products(pairs, z, ahead, archive, 1, steps - 2))
                accs = [
                    jnp.where(is_first, mine, sums[min(i + 1, steps - 3)])
                    for i, mine in enumerate(sums)
                ]
            accs = spread(pairs, z, rows_before, accs)
            own = theirs = accs[0]
            accs = accs[1:]

    early = jnp.stack(results[:-1])
    early = jnp.where(is_first, early, lax.ppermute(early, "lag", up))
    last = jnp.where(is_first, results[-1], lax.ppermute(results[-1], "lag", up))
    whole_run = jnp.concatenate([early, early[:1]], axis=0)
    return lax.dynamic_update_slice(whole_run, last[None], (steps - 1, 0, 0))


def general_body(lag_matrices, history, excitation, admittance, saturation):
    slot_count = lag_matrices.shape[0]
    step_count = excitation.shape[0]
    lag_index = lax.axis_index("lag")
    admit_col = admittance[:, None]
    satur_col = saturation[:, None]
    archive = lax.all_gather(history, "lag", axis=0, tiled=True)
    archive = lax.all_gather(archive, "row", axis=1, tiled=True)
    results = []
    for step_index in range(step_count):
        own_slots = lax.dynamic_slice_in_dim(archive, lag_index * slot_count, slot_count, 0)
        partial_sum = jnp.einsum(
            "lrm,lmc->rc", lag_matrices, own_slots, preferred_element_type=jnp.float32
        )
        summed = lax.psum(partial_sum, "lag")
        density = load_update(excitation[step_index] - summed, admit_col, satur_col)
        results.append(density)
        if step_index + 1 < step_count:
            full_density = lax.all_gather(density, "row", axis=0, tiled=True)
            archive = jnp.concatenate([full_density[None], archive[:-1]], axis=0)
    return jnp.stack(results)


def solution(mesh):
    groups, members = mesh.shape["lag"], mesh.shape["row"]
    placed = (
        P("lag", "row", None),
        P("lag", "row", None),
        P(None, "row", None),
        P("row"),
        P("row"),
    )

    def body(lag_matrices, history, excitation, admittance, saturation):
        slots, steps = lag_matrices.shape[0], excitation.shape[0]
        chosen = general_body
        depth = lag_matrices.shape[2] // members
        if groups == 2 and members % 4 == 0 and depth % 128 == 0 and 2 < steps <= slots:
            chosen = functools.partial(two_group_body, members // 2)
        return chosen(lag_matrices, history, excitation, admittance, saturation)

    return jax.shard_map(
        body, mesh=mesh, in_specs=placed, out_specs=P(None, "row", None), check_vma=False
    )
```

```python
import functools
import math

import jax
import jax.numpy as jnp
from jax import lax
from jax.experimental import pallas as pl
from jax.experimental.pallas import tpu as pltpu
from jax.sharding import PartitionSpec as P

VMEM_LIMIT = 60 * 1024 * 1024


def load_update(drive, admit_col, satur_col):
    return (admit_col * drive * lax.rsqrt(1.0 + (satur_col * drive) ** 2)).astype(jnp.bfloat16)


def ring_of(pairs):
    order = list(range(pairs))
    return order[0::2] + order[1::2][::-1]


def place_in_ring(pair, pairs):
    up, across = pair // 2, pair % 2
    return up + across * (pairs - 1 - 2 * up)


def dot(a, b):
    return jnp.dot(a, b, preferred_element_type=jnp.float32)


def call(kernel, shape, products, z_blocks, y_blocks, **kwargs):
    rows, columns, unknowns = shape
    return pl.pallas_call(
        kernel,
        compiler_params=pltpu.CompilerParams(vmem_limit_bytes=VMEM_LIMIT),
        cost_estimate=pl.CostEstimate(
            flops=2 * products * rows * unknowns * columns,
            bytes_accessed=2 * unknowns * (z_blocks * rows + y_blocks * columns),
            transcendentals=0,
        ),
        **kwargs,
    )


def add_to(out_ref, total):
    @pl.when(pl.program_id(0) == 0)
    def _():
        out_ref[...] = total

    @pl.when(pl.program_id(0) > 0)
    def _():
        out_ref[...] += total


def sizes(z, y):
    return z.shape[1], y.shape[-1], z.shape[2]


def whole(rows, columns):
    return pl.BlockSpec((rows, columns), lambda k: (0, 0))


def z_spec(rows, depth, slot):
    return pl.BlockSpec((1, rows, depth), lambda k: (slot, 0, k))


def h_spec(depth, columns, first, count, pairs):
    return pl.BlockSpec((count, depth, columns), lambda k: (first, place_in_ring(k, pairs), 0))


def y_spec(depth, columns, pairs):
    return pl.BlockSpec((depth, columns), lambda k: (place_in_ring(k, pairs), 0))


def stacked(z_refs):
    if len(z_refs) == 1:
        return z_refs[0][0]
    return jnp.concatenate([z_ref[0] for z_ref in z_refs], axis=0)


def slots_kernel(count, *refs):
    z_refs, h_ref, out_ref = refs[:count], refs[count], refs[count + 1]
    total = dot(z_refs[0][0], h_ref[0])
    for slot in range(1, count):
        total += dot(z_refs[slot][0], h_ref[slot])
    add_to(out_ref, total)


def slots_product(pairs, z, h, shift, count):
    rows, columns, unknowns = shape = sizes(z, h)
    depth = unknowns // pairs
    return call(
        functools.partial(slots_kernel, count), shape, count, count, count,
        grid=(pairs,),
        in_specs=[z_spec(rows, depth, slot) for slot in range(shift, shift + count)]
        + [h_spec(depth, columns, 0, count, pairs)],
        out_specs=whole(rows, columns),
        out_shape=jax.ShapeDtypeStruct((rows, columns), jnp.float32),
    )(*([z] * count), h)


def next_kernel(z_new_ref, y_ref, z_old_ref, h_ref, part_ref, out_ref):
    total = dot(z_new_ref[0], y_ref[...]) + dot(z_old_ref[0], h_ref[0])

    @pl.when(pl.program_id(0) == 0)
    def _():
        out_ref[...] = -part_ref[...] - total

    @pl.when(pl.program_id(0) > 0)
    def _():
        out_ref[...] -= total


def next_product(pairs, z, y, h, slot, part):
    rows, columns, unknowns = shape = sizes(z, y)
    depth = unknowns // pairs
    return call(
        next_kernel, shape, 2, 2, 2,
        grid=(pairs,),
        in_specs=[
            z_spec(rows, depth, 0),
            y_spec(depth, columns, pairs),
            z_spec(rows, depth, slot + 1),
            h_spec(depth, columns, slot, 1, pairs),
            whole(rows, columns),
        ],
        out_specs=whole(rows, columns),
        out_shape=jax.ShapeDtypeStruct((rows, columns), jnp.float32),
    )(z, y, z, h, part)


def later_kernel(rows, low, high, top, *refs):
    z_refs, y_ref, h_ref, outs, sums = refs[:top], refs[top], refs[top + 1], refs[top + 2 : -1], refs[-1]
    k = pl.program_id(0)

    @pl.when(k == 0)
    def _():
        sums[...] = jnp.zeros_like(sums)

    sums[...] -= dot(stacked(z_refs[: high - low]), y_ref[...])
    for slot in range(h_ref.shape[0]):
        stack = z_refs[slot + 1 : min(slot + 1 + high - low, top)]
        sums[: len(stack) * rows] -= dot(stacked(stack), h_ref[slot])

    @pl.when(k == pl.num_programs(0) - 1)
    def _():
        for index, out_ref in enumerate(outs):
            out_ref[...] = sums[index * rows : (index + 1) * rows]


def later_products(pairs, z, y, h, low, high):
    rows, columns, unknowns = shape = sizes(z, h)
    depth, top = unknowns // pairs, z.shape[0] - 1 - low
    count = max(top - 1, 1)
    products = high - low + sum(min(high - low, top - 1 - slot) for slot in range(top - 1))
    return call(
        functools.partial(later_kernel, rows, low, high, top), shape, products, top, count + 1,
        grid=(pairs,),
        in_specs=[z_spec(rows, depth, slot) for slot in range(low + 1, low + 1 + top)]
        + [y_spec(depth, columns, pairs), h_spec(depth, columns, 0, count, pairs)],
        out_specs=[whole(rows, columns)] * (high - low),
        out_shape=[jax.ShapeDtypeStruct((rows, columns), jnp.float32)] * (high - low),
        scratch_shapes=[pltpu.VMEM(((high - low) * rows, columns), jnp.float32)],
    )(*([z] * top), y, h)


def spread_kernel(rows, count, *refs):
    z_refs, y_ref = refs[:count], refs[count]
    accs, outs = refs[count + 1 : 2 * count + 1], refs[2 * count + 1 :]
    total = dot(stacked(z_refs), y_ref[...])
    for index in range(count):
        term = total[index * rows : (index + 1) * rows]

        @pl.when(pl.program_id(0) == 0)
        def _():
            outs[index][...] = accs[index][...] - term

        @pl.when(pl.program_id(0) > 0)
        def _():
            outs[index][...] -= term


def spread(pairs, z, y, accs):
    rows, columns, unknowns = shape = sizes(z, y)
    depth, count = unknowns // pairs, len(accs)
    return call(
        functools.partial(spread_kernel, rows, count), shape, count, count, 1,
        grid=(pairs,),
        in_specs=[z_spec(rows, depth, slot) for slot in range(1, 1 + count)]
        + [y_spec(depth, columns, pairs)]
        + [whole(rows, columns)] * count,
        out_specs=[whole(rows, columns)] * count,
        out_shape=[jax.ShapeDtypeStruct((rows, columns), jnp.float32)] * count,
    )(*([z] * count), y, *accs)


def step_kernel(
    pairs, last, flag_ref, z_ref, y_ref, base_ref, next_ref, loads_ref, send_ref, drive_ref,
    z_buf, y_buf, base_buf, next_buf, loads_buf, drive_buf, send_buf, z_sems, y_sems, sems,
):
    depth = z_buf.shape[1] // pairs
    copies = []
    for at, pair in enumerate(ring_of(pairs)):
        across, down = pl.ds(pair * depth, depth), pl.ds(at * depth, depth)
        copies.append((
            pltpu.make_async_copy(z_ref.at[0, :, across], z_buf.at[:, across], z_sems.at[at]),
            pltpu.make_async_copy(y_ref.at[down, :], y_buf.at[down, :], y_sems.at[at]),
        ))
    for z_copy, y_copy in copies:
        z_copy.start()
        y_copy.start()
    small = [
        pltpu.make_async_copy(base_ref, base_buf, sems.at[0]),
        pltpu.make_async_copy(next_ref, next_buf, sems.at[1]),
        pltpu.make_async_copy(loads_ref, loads_buf, sems.at[2]),
    ]
    for copy in small:
        copy.start()
    for at, pair in enumerate(ring_of(pairs)):
        for copy in copies[at]:
            copy.wait()
        term = dot(z_buf[:, pair * depth : (pair + 1) * depth], y_buf[at * depth : (at + 1) * depth])
        if at == 0:
            drive_buf[...] = term
        else:
            drive_buf[...] += term
    for copy in small:
        copy.wait()
    drive_buf[...] = base_buf[...] - drive_buf[...]
    if not last:
        drive_copy = pltpu.make_async_copy(drive_buf, drive_ref, sems.at[3])
        drive_copy.start()
    first = flag_ref[0] != 0
    lanes = loads_buf.shape[2]
    for start in range(0, drive_buf.shape[1], lanes):
        part = pl.ds(start, lanes)
        density = load_update(drive_buf[:, part], loads_buf[0], loads_buf[1])
        send_buf[:, part] = jnp.where(first, density, next_buf[:, part])
    send_copy = pltpu.make_async_copy(send_buf, send_ref, sems.at[4])
    send_copy.start()
    send_copy.wait()
    if not last:
        drive_copy.wait()


def last_step_kernel(pairs, *refs):
    step_kernel(pairs, True, *refs[:7], None, *refs[7:])


def step(pairs, flag, z, y, base, following, loads, last):
    rows, columns, unknowns = shape = sizes(z, y)
    hbm = pl.BlockSpec(memory_space=pl.ANY)
    outs = [
        jax.ShapeDtypeStruct((rows, columns), jnp.bfloat16),
        jax.ShapeDtypeStruct((rows, columns), jnp.float32),
    ]
    kernel = functools.partial(step_kernel, pairs, False)
    if last:
        kernel, outs = functools.partial(last_step_kernel, pairs), outs[:1]
    return call(
        kernel, shape, 1, 1, 1,
        in_specs=[pl.BlockSpec(memory_space=pltpu.SMEM)] + [hbm] * 5,
        out_specs=[hbm] * len(outs),
        out_shape=outs,
        scratch_shapes=[
            pltpu.VMEM((rows, unknowns), jnp.bfloat16),
            pltpu.VMEM((unknowns, columns), jnp.bfloat16),
            pltpu.VMEM((rows, columns), jnp.float32),
            pltpu.VMEM((rows, columns), jnp.bfloat16),
            pltpu.VMEM(loads.shape, jnp.float32),
            pltpu.VMEM((rows, columns), jnp.float32),
            pltpu.VMEM((rows, columns), jnp.bfloat16),
            pltpu.SemaphoreType.DMA((pairs,)),
            pltpu.SemaphoreType.DMA((pairs,)),
            pltpu.SemaphoreType.DMA((5,)),
        ],
    )(flag, z, y, base, following, loads)


def gather_rows(pairs, block, axis):
    order = [2 * pair + core for pair in ring_of(pairs) for core in (0, 1)]
    return lax.all_gather(block, "row", axis=axis, tiled=True, axis_index_groups=[order])


def two_group_body(pairs, lag_matrices, history, excitation, admittance, saturation):
    z, steps = lag_matrices, excitation.shape[0]
    slots = z.shape[0]
    is_first = lax.axis_index("lag") == 0
    flag = is_first.astype(jnp.int32)[None]
    admit_col, satur_col = admittance[:, None], saturation[:, None]
    lanes = math.gcd(128, excitation.shape[-1])
    loads = jnp.broadcast_to(jnp.stack([admit_col, satur_col]), (2, admit_col.shape[0], lanes))
    down, up = [(1, 0)], [(0, 1)]

    incoming = lax.ppermute(history[slots - (steps - 1) :], "lag", up)
    archive = gather_rows(pairs, history, 1)
    archive, *incoming = lax.optimization_barrier((archive, *incoming))
    ahead = gather_rows(pairs, incoming[steps - 2], 0)

    first_part = slots_product(pairs, z, archive, 0, slots)
    first_other = lax.ppermute(first_part, "lag", down)
    archive, first_part = lax.optimization_barrier((archive, first_part))
    part = slots_product(pairs, z, archive, 1, slots - 2)
    part, first_part = lax.optimization_barrier((part, first_part))
    density = load_update(excitation[0] - (first_part + first_other), admit_col, satur_col)
    send = jnp.where(is_first, density, incoming[steps - 3])
    results = [send]
    fresh = gather_rows(pairs, send, 0)

    ahead, send = lax.optimization_barrier((ahead, send))
    own = next_product(pairs, z, ahead, archive, slots - 2, part)
    other = lax.ppermute(own, "lag", down)
    archive, own = lax.optimization_barrier((archive, own))
    (theirs,) = later_products(pairs, z, ahead, archive, 0, 1)
    theirs, loads = lax.optimization_barrier((theirs, loads))
    accs = []

    for index in range(1, steps):
        base = jnp.where(is_first, excitation[index] + other + own, theirs)
        coming = incoming[max(steps - 3 - index, 0)]
        send, *drive = step(pairs, flag, z, fresh, base, coming, loads, index + 1 == steps)
        results.append(send)
        if index + 1 < steps:
            rows_before = fresh
            fresh = gather_rows(pairs, send, 0)
            other = lax.ppermute(drive[0], "lag", down)
            rows_before, ahead, archive, send = lax.optimization_barrier(
                (rows_before, ahead, archive, send)
            )
            if index == 1:
                sums = [theirs] + list(later_products(pairs, z, ahead, archive, 1, steps - 2))
                accs = [
                    jnp.where(is_first, mine, sums[min(i + 1, steps - 3)])
                    for i, mine in enumerate(sums)
                ]
            accs = spread(pairs, z, rows_before, accs)
            own = theirs = accs[0]
            accs = accs[1:]

    early = jnp.stack(results[:-1])
    early = jnp.where(is_first, early, lax.ppermute(early, "lag", up))
    last = jnp.where(is_first, results[-1], lax.ppermute(results[-1], "lag", up))
    whole_run = jnp.concatenate([early, early[:1]], axis=0)
    return lax.dynamic_update_slice(whole_run, last[None], (steps - 1, 0, 0))


def general_body(lag_matrices, history, excitation, admittance, saturation):
    slot_count = lag_matrices.shape[0]
    step_count = excitation.shape[0]
    lag_index = lax.axis_index("lag")
    admit_col = admittance[:, None]
    satur_col = saturation[:, None]
    archive = lax.all_gather(history, "lag", axis=0, tiled=True)
    archive = lax.all_gather(archive, "row", axis=1, tiled=True)
    results = []
    for step_index in range(step_count):
        own_slots = lax.dynamic_slice_in_dim(archive, lag_index * slot_count, slot_count, 0)
        partial_sum = jnp.einsum(
            "lrm,lmc->rc", lag_matrices, own_slots, preferred_element_type=jnp.float32
        )
        summed = lax.psum(partial_sum, "lag")
        density = load_update(excitation[step_index] - summed, admit_col, satur_col)
        results.append(density)
        if step_index + 1 < step_count:
            full_density = lax.all_gather(density, "row", axis=0, tiled=True)
            archive = jnp.concatenate([full_density[None], archive[:-1]], axis=0)
    return jnp.stack(results)


def solution(mesh):
    groups, members = mesh.shape["lag"], mesh.shape["row"]
    placed = (
        P("lag", "row", None),
        P("lag", "row", None),
        P(None, "row", None),
        P("row"),
        P("row"),
    )

    def body(lag_matrices, history, excitation, admittance, saturation):
        slots, steps = lag_matrices.shape[0], excitation.shape[0]
        chosen = general_body
        depth = lag_matrices.shape[2] // members
        if groups == 2 and members % 4 == 0 and depth % 128 == 0 and 3 < steps <= slots:
            chosen = functools.partial(two_group_body, members // 2)
        return chosen(lag_matrices, history, excitation, admittance, saturation)

    return jax.shard_map(
        body, mesh=mesh, in_specs=placed, out_specs=P(None, "row", None), check_vma=False
    )
```

```python
import functools
import math

import jax
import jax.numpy as jnp
from jax import lax
from jax.experimental import pallas as pl
from jax.experimental.pallas import tpu as pltpu
from jax.sharding import PartitionSpec as P

VMEM_LIMIT = 60 * 1024 * 1024


def load_update(drive, admit_col, satur_col):
    return (admit_col * drive * lax.rsqrt(1.0 + (satur_col * drive) ** 2)).astype(jnp.bfloat16)


def ring_of(pairs):
    order = list(range(pairs))
    return order[0::2] + order[1::2][::-1]


def place_in_ring(pair, pairs):
    up, across = pair // 2, pair % 2
    return up + across * (pairs - 1 - 2 * up)


def dot(a, b):
    return jnp.dot(a, b, preferred_element_type=jnp.float32)


def call(kernel, shape, products, z_blocks, y_blocks, **kwargs):
    rows, columns, unknowns = shape
    return pl.pallas_call(
        kernel,
        compiler_params=pltpu.CompilerParams(vmem_limit_bytes=VMEM_LIMIT),
        cost_estimate=pl.CostEstimate(
            flops=2 * products * rows * unknowns * columns,
            bytes_accessed=2 * unknowns * (z_blocks * rows + y_blocks * columns),
            transcendentals=0,
        ),
        **kwargs,
    )


def add_to(out_ref, total):
    @pl.when(pl.program_id(0) == 0)
    def _():
        out_ref[...] = total

    @pl.when(pl.program_id(0) > 0)
    def _():
        out_ref[...] += total


def sizes(z, y):
    return z.shape[1], y.shape[-1], z.shape[2]


def whole(rows, columns):
    return pl.BlockSpec((rows, columns), lambda k: (0, 0))


def z_spec(rows, depth, slot):
    return pl.BlockSpec((1, rows, depth), lambda k: (slot, 0, k))


def h_spec(depth, columns, first, count, pairs):
    return pl.BlockSpec((count, depth, columns), lambda k: (first, place_in_ring(k, pairs), 0))


def y_spec(depth, columns, pairs):
    return pl.BlockSpec((depth, columns), lambda k: (place_in_ring(k, pairs), 0))


def stacked(z_refs):
    if len(z_refs) == 1:
        return z_refs[0][0]
    return jnp.concatenate([z_ref[0] for z_ref in z_refs], axis=0)


def slots_kernel(count, *refs):
    z_refs, h_ref, out_ref = refs[:-2], refs[-2], refs[-1]
    blocks = [z_ref.at[slot] for z_ref in z_refs for slot in range(z_ref.shape[0])]
    total = dot(blocks[0][...], h_ref[0])
    for slot in range(1, count):
        total += dot(blocks[slot][...], h_ref[slot])
    add_to(out_ref, total)


def slots_product(pairs, z, h, shift, count):
    rows, columns, unknowns = shape = sizes(z, h)
    depth = unknowns // pairs
    z_specs = [z_spec(rows, depth, slot) for slot in range(shift, shift + count)]
    if shift == 0:
        z_specs = [pl.BlockSpec((count, rows, depth), lambda k: (0, 0, k))]
    return call(
        functools.partial(slots_kernel, count), shape, count, count, count,
        grid=(pairs,),
        in_specs=z_specs + [h_spec(depth, columns, 0, count, pairs)],
        out_specs=whole(rows, columns),
        out_shape=jax.ShapeDtypeStruct((rows, columns), jnp.float32),
    )(*([z] * len(z_specs)), h)


def next_kernel(z_new_ref, y_ref, z_old_ref, h_ref, part_ref, out_ref):
    total = dot(z_new_ref[0], y_ref[...]) + dot(z_old_ref[0], h_ref[0])

    @pl.when(pl.program_id(0) == 0)
    def _():
        out_ref[...] = -part_ref[...] - total

    @pl.when(pl.program_id(0) > 0)
    def _():
        out_ref[...] -= total


def next_product(pairs, z, y, h, slot, part):
    rows, columns, unknowns = shape = sizes(z, y)
    depth = unknowns // pairs
    return call(
        next_kernel, shape, 2, 2, 2,
        grid=(pairs,),
        in_specs=[
            z_spec(rows, depth, 0),
            y_spec(depth, columns, pairs),
            z_spec(rows, depth, slot + 1),
            h_spec(depth, columns, slot, 1, pairs),
            whole(rows, columns),
        ],
        out_specs=whole(rows, columns),
        out_shape=jax.ShapeDtypeStruct((rows, columns), jnp.float32),
    )(z, y, z, h, part)


def later_kernel(rows, low, high, top, *refs):
    z_refs, y_ref, h_ref, outs, sums = refs[:top], refs[top], refs[top + 1], refs[top + 2 : -1], refs[-1]
    k = pl.program_id(0)

    @pl.when(k == 0)
    def _():
        sums[...] = jnp.zeros_like(sums)

    sums[...] -= dot(stacked(z_refs[: high - low]), y_ref[...])
    for slot in range(h_ref.shape[0]):
        stack = z_refs[slot + 1 : min(slot + 1 + high - low, top)]
        sums[: len(stack) * rows] -= dot(stacked(stack), h_ref[slot])

    @pl.when(k == pl.num_programs(0) - 1)
    def _():
        for index, out_ref in enumerate(outs):
            out_ref[...] = sums[index * rows : (index + 1) * rows]


def later_products(pairs, z, y, h, low, high):
    rows, columns, unknowns = shape = sizes(z, h)
    depth, top = unknowns // pairs, z.shape[0] - 1 - low
    count = max(top - 1, 1)
    products = high - low + sum(min(high - low, top - 1 - slot) for slot in range(top - 1))
    return call(
        functools.partial(later_kernel, rows, low, high, top), shape, products, top, count + 1,
        grid=(pairs,),
        in_specs=[z_spec(rows, depth, slot) for slot in range(low + 1, low + 1 + top)]
        + [y_spec(depth, columns, pairs), h_spec(depth, columns, 0, count, pairs)],
        out_specs=[whole(rows, columns)] * (high - low),
        out_shape=[jax.ShapeDtypeStruct((rows, columns), jnp.float32)] * (high - low),
        scratch_shapes=[pltpu.VMEM(((high - low) * rows, columns), jnp.float32)],
    )(*([z] * top), y, h)


def spread_kernel(rows, count, *refs):
    z_refs, y_ref = refs[:count], refs[count]
    accs, outs = refs[count + 1 : 2 * count + 1], refs[2 * count + 1 :]
    total = dot(stacked(z_refs), y_ref[...])
    for index in range(count):
        term = total[index * rows : (index + 1) * rows]

        @pl.when(pl.program_id(0) == 0)
        def _():
            outs[index][...] = accs[index][...] - term

        @pl.when(pl.program_id(0) > 0)
        def _():
            outs[index][...] -= term


def spread(pairs, z, y, accs):
    rows, columns, unknowns = shape = sizes(z, y)
    depth, count = unknowns // pairs, len(accs)
    return call(
        functools.partial(spread_kernel, rows, count), shape, count, count, 1,
        grid=(pairs,),
        in_specs=[z_spec(rows, depth, slot) for slot in range(1, 1 + count)]
        + [y_spec(depth, columns, pairs)]
        + [whole(rows, columns)] * count,
        out_specs=[whole(rows, columns)] * count,
        out_shape=[jax.ShapeDtypeStruct((rows, columns), jnp.float32)] * count,
    )(*([z] * count), y, *accs)


def step_kernel(
    pairs, flag_ref, z_ref, y_ref, base_ref, next_ref, loads_ref, drive_ref, send_ref,
    z_buf, y_buf, base_buf, next_buf, loads_buf, drive_buf, send_buf, z_sems, y_sems, sems,
):
    depth = z_buf.shape[1] // pairs
    copies = []
    for at, pair in enumerate(ring_of(pairs)):
        across, down = pl.ds(pair * depth, depth), pl.ds(at * depth, depth)
        copies.append((
            pltpu.make_async_copy(z_ref.at[0, :, across], z_buf.at[:, across], z_sems.at[at]),
            pltpu.make_async_copy(y_ref.at[down, :], y_buf.at[down, :], y_sems.at[at]),
        ))
    for z_copy, y_copy in copies:
        z_copy.start()
        y_copy.start()
    small = [
        pltpu.make_async_copy(base_ref, base_buf, sems.at[0]),
        pltpu.make_async_copy(next_ref, next_buf, sems.at[1]),
        pltpu.make_async_copy(loads_ref, loads_buf, sems.at[2]),
    ]
    for copy in small:
        copy.start()
    for at, pair in enumerate(ring_of(pairs)):
        for copy in copies[at]:
            copy.wait()
        term = dot(z_buf[:, pair * depth : (pair + 1) * depth], y_buf[at * depth : (at + 1) * depth])
        if at == 0:
            drive_buf[...] = term
        else:
            drive_buf[...] += term
    for copy in small:
        copy.wait()
    drive_buf[...] = base_buf[...] - drive_buf[...]
    drive_copy = pltpu.make_async_copy(drive_buf, drive_ref, sems.at[3])
    drive_copy.start()
    first = flag_ref[0] != 0
    lanes = loads_buf.shape[2]
    for start in range(0, drive_buf.shape[1], lanes):
        part = pl.ds(start, lanes)
        density = load_update(drive_buf[:, part], loads_buf[0], loads_buf[1])
        send_buf[:, part] = jnp.where(first, density, next_buf[:, part])
    send_copy = pltpu.make_async_copy(send_buf, send_ref, sems.at[4])
    send_copy.start()
    send_copy.wait()
    drive_copy.wait()


def step(pairs, flag, z, y, base, following, loads):
    rows, columns, unknowns = shape = sizes(z, y)
    hbm = pl.BlockSpec(memory_space=pl.ANY)
    return call(
        functools.partial(step_kernel, pairs), shape, 1, 1, 1,
        in_specs=[pl.BlockSpec(memory_space=pltpu.SMEM)] + [hbm] * 5,
        out_specs=[hbm, hbm],
        out_shape=[
            jax.ShapeDtypeStruct((rows, columns), jnp.float32),
            jax.ShapeDtypeStruct((rows, columns), jnp.bfloat16),
        ],
        scratch_shapes=[
            pltpu.VMEM((rows, unknowns), jnp.bfloat16),
            pltpu.VMEM((unknowns, columns), jnp.bfloat16),
            pltpu.VMEM((rows, columns), jnp.float32),
            pltpu.VMEM((rows, columns), jnp.bfloat16),
            pltpu.VMEM(loads.shape, jnp.float32),
            pltpu.VMEM((rows, columns), jnp.float32),
            pltpu.VMEM((rows, columns), jnp.bfloat16),
            pltpu.SemaphoreType.DMA((pairs,)),
            pltpu.SemaphoreType.DMA((pairs,)),
            pltpu.SemaphoreType.DMA((5,)),
        ],
    )(flag, z, y, base, following, loads)


def gather_rows(pairs, block, axis):
    order = [2 * pair + core for pair in ring_of(pairs) for core in (0, 1)]
    return lax.all_gather(block, "row", axis=axis, tiled=True, axis_index_groups=[order])


def two_group_body(pairs, lag_matrices, history, excitation, admittance, saturation):
    z, steps = lag_matrices, excitation.shape[0]
    slots = z.shape[0]
    is_first = lax.axis_index("lag") == 0
    flag = is_first.astype(jnp.int32)[None]
    admit_col, satur_col = admittance[:, None], saturation[:, None]
    lanes = math.gcd(128, excitation.shape[-1])
    loads = jnp.broadcast_to(jnp.stack([admit_col, satur_col]), (2, admit_col.shape[0], lanes))
    down, up = [(1, 0)], [(0, 1)]

    incoming = lax.ppermute(history[slots - (steps - 1) :], "lag", up)
    archive = gather_rows(pairs, history, 1)
    archive, *incoming = lax.optimization_barrier((archive, *incoming))
    ahead = gather_rows(pairs, incoming[steps - 2], 0)

    first_part = slots_product(pairs, z, archive, 0, slots)
    first_other = lax.ppermute(first_part, "lag", down)
    archive, first_part = lax.optimization_barrier((archive, first_part))
    part = slots_product(pairs, z, archive, 1, slots - 2)
    part, first_part = lax.optimization_barrier((part, first_part))
    density = load_update(excitation[0] - (first_part + first_other), admit_col, satur_col)
    send = jnp.where(is_first, density, incoming[steps - 3])
    results = [send]
    fresh = gather_rows(pairs, send, 0)

    ahead, send = lax.optimization_barrier((ahead, send))
    own = next_product(pairs, z, ahead, archive, slots - 2, part)
    other = lax.ppermute(own, "lag", down)
    archive, own = lax.optimization_barrier((archive, own))
    (theirs,) = later_products(pairs, z, ahead, archive, 0, 1)
    theirs, loads = lax.optimization_barrier((theirs, loads))
    accs = []

    for index in range(1, steps):
        base = jnp.where(is_first, excitation[index] + other + own, theirs)
        coming = incoming[max(steps - 3 - index, 0)]
        drive, send = step(pairs, flag, z, fresh, base, coming, loads)
        results.append(send)
        if index + 1 < steps:
            rows_before = fresh
            fresh = gather_rows(pairs, send, 0)
            other = lax.ppermute(drive, "lag", down)
            rows_before, ahead, archive, send = lax.optimization_barrier(
                (rows_before, ahead, archive, send)
            )
            if index == 1:
                sums = [theirs] + list(later_products(pairs, z, ahead, archive, 1, steps - 2))
                accs = [
                    jnp.where(is_first, mine, sums[min(i + 1, steps - 3)])
                    for i, mine in enumerate(sums)
                ]
            accs = spread(pairs, z, rows_before, accs)
            own = theirs = accs[0]
            accs = accs[1:]

    early = jnp.stack(results[:-1])
    early = jnp.where(is_first, early, lax.ppermute(early, "lag", up))
    last = jnp.where(is_first, results[-1], lax.ppermute(results[-1], "lag", up))
    whole_run = jnp.concatenate([early, early[:1]], axis=0)
    return lax.dynamic_update_slice(whole_run, last[None], (steps - 1, 0, 0))


def general_body(lag_matrices, history, excitation, admittance, saturation):
    slot_count = lag_matrices.shape[0]
    step_count = excitation.shape[0]
    lag_index = lax.axis_index("lag")
    admit_col = admittance[:, None]
    satur_col = saturation[:, None]
    archive = lax.all_gather(history, "lag", axis=0, tiled=True)
    archive = lax.all_gather(archive, "row", axis=1, tiled=True)
    results = []
    for step_index in range(step_count):
        own_slots = lax.dynamic_slice_in_dim(archive, lag_index * slot_count, slot_count, 0)
        partial_sum = jnp.einsum(
            "lrm,lmc->rc", lag_matrices, own_slots, preferred_element_type=jnp.float32
        )
        summed = lax.psum(partial_sum, "lag")
        density = load_update(excitation[step_index] - summed, admit_col, satur_col)
        results.append(density)
        if step_index + 1 < step_count:
            full_density = lax.all_gather(density, "row", axis=0, tiled=True)
            archive = jnp.concatenate([full_density[None], archive[:-1]], axis=0)
    return jnp.stack(results)


def solution(mesh):
    groups, members = mesh.shape["lag"], mesh.shape["row"]
    placed = (
        P("lag", "row", None),
        P("lag", "row", None),
        P(None, "row", None),
        P("row"),
        P("row"),
    )

    def body(lag_matrices, history, excitation, admittance, saturation):
        slots, steps = lag_matrices.shape[0], excitation.shape[0]
        chosen = general_body
        depth = lag_matrices.shape[2] // members
        if groups == 2 and members % 4 == 0 and depth % 128 == 0 and 3 < steps <= slots:
            chosen = functools.partial(two_group_body, members // 2)
        return chosen(lag_matrices, history, excitation, admittance, saturation)

    return jax.shard_map(
        body, mesh=mesh, in_specs=placed, out_specs=P(None, "row", None), check_vma=False
    )
```
